32 devices in a mesh: replica: 8 (over y, x, core), fsdp: 4 (over z).
Axes of the slice: x: 2, y: 2, z: 4, core: 2. Of those that a mesh axis runs over, the one named last changes fastest.
Arguments:
- activations: bfloat16 [8, 512, 8192], P('replica', 'fsdp'), may hold values from -6 to 6
- key_grad: bfloat16 [8, 512, 512], P('replica', 'fsdp'), may hold values from -6 to 6
- inner_weight: bfloat16 [8, 512, 8192], P('replica', None, 'fsdp'), may hold values from -4 to 4
- weight_first: bfloat16 [8, 512, 8192], P('replica', None, 'fsdp'), may hold values from -0.14941406 to 0.14941406
- weight_second: bfloat16 [8, 512, 8192], P('replica', None, 'fsdp'), may hold values from 0.00062179565 to 0.012451172
- norm_gain: float32 [8, 8192], P('replica', 'fsdp'), may hold values from 0.1 to 1.9
- gain_first: float32 [8, 8192], P('replica', 'fsdp'), may hold values from -10 to 10
- gain_second: float32 [8, 8192], P('replica', 'fsdp'), may hold values from 10 to 200
- step_count: int32 [], replicated, may hold values from 1 to 19
- outer_params: float32 [512, 8192], P('replica', 'fsdp'), may hold values from -4 to 4
- outer_momentum: float32 [512, 8192], P('replica', 'fsdp'), may hold values from -3 to 3
Outputs:
- merged_weight: bfloat16 [8, 512, 8192], P('replica', None, 'fsdp')
- outer_params_new: float32 [512, 8192], P('replica', 'fsdp')
- outer_momentum_new: float32 [512, 8192], P('replica', 'fsdp')
- gain_new: float32 [8, 8192], P('replica', 'fsdp')
- gain_first_new: float32 [8, 8192], P('replica', 'fsdp')
- gain_second_new: float32 [8, 8192], P('replica', 'fsdp')
The draws below stay inside these ranges and needn't reach their ends.
All inputs are finite; a program needn't handle non-finite values.
Results may differ from the reference program's by a relative error of at most 0.008.
Values may be sent and summed in bfloat16 or wider, within the bound.
A program may use at most 128 MiB of HBM per device.

```python
import math
import jax
import jax.numpy as jnp
from jax import lax

D = 8192
KEY_WIDTH = 512
GROUP_TOK = 512
REPLICAS = 8
N_REPLICA = 8


def shard_levels(key, extent, shards, low, top_value):
    factor_of, own = 1.0, jax.random.fold_in(key, 6)
    for axis_at, shards_of in shards:
        heights = jnp.exp(jax.random.uniform(jax.random.fold_in(own, axis_at), (shards_of,), jnp.float32, low / len(shards), top_value / len(shards)))
        factor_of = factor_of * jnp.repeat(heights, extent[axis_at] // shards_of).reshape([-1 if axis == axis_at else 1 for axis in range(len(extent))])
    return factor_of


def centred(stream_key, dims, deviation, most, cuts=(), held_as=jnp.bfloat16):
    drawn = deviation * jax.random.normal(stream_key, dims, jnp.float32)
    if cuts:
        drawn = drawn * shard_levels(stream_key, dims, cuts, -0.22, 0.18)
    return jnp.clip(drawn, -most, most).astype(held_as)


def setup_inputs(seed: int = 0) -> dict:
    streams_of = jax.random.split(jax.random.key(seed), 12)
    activations = centred(streams_of[0], (REPLICAS, GROUP_TOK, D), 1.0, 6.0, ((0, 8), (1, 4)))
    key_grad = centred(streams_of[1], (REPLICAS, GROUP_TOK, KEY_WIDTH), 1.0, 6.0, ((0, 8), (1, 4)))
    inner_weight = centred(streams_of[2], (REPLICAS, KEY_WIDTH, D), 1.0, 4.0, ((0, 8), (2, 4)))
    weight_first = centred(streams_of[3], (REPLICAS, KEY_WIDTH, D), (0.1 * (GROUP_TOK * D ** -1) ** 0.5), 0.14941406, ((0, 8), (2, 4)))
    weight_second = jnp.clip(jnp.exp(math.log(0.012451172) - 2.9969585 * jax.random.uniform(streams_of[4], (REPLICAS, KEY_WIDTH, D), jnp.float32) ** shard_levels(streams_of[4], (REPLICAS, KEY_WIDTH, D), ((0, 8), (2, 4)), -0.2, 0.2)), 0.00062179565, 0.012451172).astype(jnp.bfloat16)
    norm_gain = jnp.clip(1.0 + 0.18 * jax.random.normal(streams_of[5], (REPLICAS, D), jnp.float32), 0.1, 1.9)
    gain_first = centred(streams_of[6], (REPLICAS, D), 2.0, 10.0, ((0, 8), (1, 4)), jnp.float32)
    gain_second = jnp.clip(jnp.exp(math.log(200.0) - 2.9957323 * jax.random.uniform(streams_of[7], (REPLICAS, D), jnp.float32) ** shard_levels(streams_of[7], (REPLICAS, D), ((0, 8), (1, 4)), -0.2, 0.2)), 10.0, 200.0)
    step_count = jax.random.randint(streams_of[8], (), 1, 20).astype(jnp.int32)
    outer_params = centred(streams_of[9], (KEY_WIDTH, D), 1.0, 4.0, ((0, 8), (1, 4)), jnp.float32)
    outer_momentum = centred(streams_of[10], (KEY_WIDTH, D), 0.5, 3.0, ((0, 8), (1, 4)), jnp.float32)
    return dict(activations=activations, key_grad=key_grad, inner_weight=inner_weight, weight_first=weight_first, weight_second=weight_second, norm_gain=norm_gain, gain_first=gain_first, gain_second=gain_second, step_count=step_count, outer_params=outer_params, outer_momentum=outer_momentum)


BETA_ONE = 0.9
BETA_TWO = 0.95
ADAM_EPS = 1e-08
INNER_RATE = 0.25
WEIGHT_DECAY = 0.1
OUTER_RATE = 0.7
OUTER_MOMENTUM = 0.9
MIX_LOCAL = 0.5
NORM_EPS = 1e-05

def adamw(param, gradient, first_moment, second_moment, correct_first, correct_second, decay):
    first_new = BETA_ONE * first_moment + (1.0 - BETA_ONE) * gradient
    second_new = BETA_TWO * second_moment + (1.0 - BETA_TWO) * gradient * gradient
    update = first_new / correct_first / (jnp.sqrt(second_new / correct_second) + ADAM_EPS) + decay * param
    return (param - INNER_RATE * update, first_new, second_new)

def nesterov(params, momentum, average):
    change = params - average
    momentum_new = OUTER_MOMENTUM * momentum + change
    return (params - OUTER_RATE * (change + OUTER_MOMENTUM * momentum_new), momentum_new)

def reference(activations, key_grad, inner_weight, weight_first, weight_second, norm_gain, gain_first, gain_second, step_count, outer_params, outer_momentum):
    step_value = step_count.astype(jnp.float32)
    correct_first = 1.0 - jnp.power(jnp.float32(BETA_ONE), step_value)
    correct_second = 1.0 - jnp.power(jnp.float32(BETA_TWO), step_value)
    factor = D ** (-0.5)
    average = lax.optimization_barrier(jnp.sum(inner_weight, axis=0, dtype=jnp.float32)) / N_REPLICA
    params_new, momentum_new = nesterov(outer_params, outer_momentum, average)

    def one_replica(bundle):
        inputs, cotangent, weight, first_moment, second_moment, gain, gfirst, gsecond = bundle
        token_rows = inputs.astype(jnp.float32)
        normed = (token_rows * lax.rsqrt(lax.optimization_barrier(jnp.mean(token_rows * token_rows, axis=1, keepdims=True)) + NORM_EPS)).astype(jnp.bfloat16)
        shaped = (normed.astype(jnp.float32) * gain).astype(jnp.bfloat16)
        weight_grad = lax.dot_general(cotangent, shaped, (((0,), (0,)), ((), ())), preferred_element_type=jnp.float32) * factor
        input_grad = jnp.dot(cotangent, weight, preferred_element_type=jnp.float32)
        gain_grad = lax.optimization_barrier(jnp.sum(input_grad * normed.astype(jnp.float32), axis=0)) * factor
        local_weight, unused_first, unused_second = adamw(weight.astype(jnp.float32), weight_grad, first_moment.astype(jnp.float32), second_moment.astype(jnp.float32), correct_first, correct_second, WEIGHT_DECAY)
        gain_out, gain_first_out, gain_second_out = adamw(gain, gain_grad, gfirst, gsecond, correct_first, correct_second, 0.0)
        merged = (MIX_LOCAL * local_weight + (1.0 - MIX_LOCAL) * params_new).astype(jnp.bfloat16)
        return (merged, gain_out, gain_first_out, gain_second_out)
    merged_weight, gain_new, gain_first_new, gain_second_new = lax.map(one_replica, (activations, key_grad, inner_weight, weight_first, weight_second, norm_gain, gain_first, gain_second))
    return (merged_weight, params_new, momentum_new, gain_new, gain_first_new, gain_second_new)
```

```python
import functools
import math

import jax
import jax.numpy as jnp
from jax import lax
from jax.experimental import pallas as pl
from jax.experimental.pallas import tpu as pltpu
from jax.sharding import PartitionSpec as P

BETA_ONE = 0.9
BETA_TWO = 0.95
ADAM_EPS = 1e-08
INNER_RATE = 0.25
WEIGHT_DECAY = 0.1
OUTER_RATE = 0.7
OUTER_MOMENTUM = 0.9
MIX_LOCAL = 0.5
NORM_EPS = 1e-05

MESH = pl.DeviceIdType.MESH
F32 = jnp.float32
BF16 = jnp.bfloat16


def kernel(
    n_f,
    n_r,
    chunk,
    step_ref,
    act,
    key,
    weight,
    first,
    second,
    gain,
    gfirst,
    gsecond,
    outer,
    momentum,
    merged_out,
    outer_out,
    momentum_out,
    gain_out,
    gfirst_out,
    gsecond_out,
    x_own,
    x_all,
    k_own,
    k_scaled,
    k_all,
    w_buf,
    m_buf,
    v_buf,
    g_buf,
    merged,
    pair_in,
    pair_sum,
    rs_in,
    par_all,
    outer_buf,
    mom_buf,
    outer_new,
    mom_new,
    gains,
    gains_new,
    local_sem,
    out_sem,
    act_send,
    act_recv,
    k_send,
    k_recv,
    pair_send,
    pair_recv,
    rs_send,
    rs_recv,
    ag_send,
    ag_recv,
    fw_send,
    fw_recv,
):
    tokens = act.shape[1]
    width = act.shape[2]
    cols = weight.shape[2]
    features = weight.shape[1]
    rows = outer.shape[0]
    chunks = cols // chunk
    chips = n_r // 2
    factor = width ** (-0.5)

    me_f = lax.axis_index("fsdp")
    me_r = lax.axis_index("replica")
    chip, core = me_r // 2, me_r % 2
    mate = chip * 2 + 1 - core

    def peer_f(offset):
        return lax.rem(me_f + offset + n_f, n_f)

    def peer_chip(offset):
        return lax.rem(chip + offset + chips, chips)

    def to_f(index):
        return (me_r, index)

    def to_r(index):
        return (index, me_f)

    def row_block(index):
        return pl.ds(pl.multiple_of(index * rows, rows), rows)

    def tok_block(index):
        return pl.ds(pl.multiple_of(index * tokens, tokens), tokens)

    def chunk_cols(j):
        return pl.ds(pl.multiple_of(j * chunk, chunk), chunk)

    loads = [
        pltpu.make_async_copy(act.at[0], x_own, local_sem.at[0]),
        pltpu.make_async_copy(key.at[0], k_own, local_sem.at[1]),
        pltpu.make_async_copy(weight.at[0], w_buf, local_sem.at[2]),
        pltpu.make_async_copy(outer, outer_buf, local_sem.at[3]),
        pltpu.make_async_copy(momentum, mom_buf, local_sem.at[4]),
        pltpu.make_async_copy(
            act.at[0, :, pl.ds(pl.multiple_of(me_f * cols, cols), cols)],
            x_all.at[tok_block(me_f), :],
            local_sem.at[5],
        ),
        pltpu.make_async_copy(first.at[0], m_buf, local_sem.at[6]),
        pltpu.make_async_copy(second.at[0], v_buf, local_sem.at[7]),
        pltpu.make_async_copy(gain, gains.at[0], local_sem.at[8]),
        pltpu.make_async_copy(gfirst, gains.at[1], local_sem.at[9]),
        pltpu.make_async_copy(gsecond, gains.at[2], local_sem.at[10]),
    ]
    for load in loads:
        load.start()

    barrier = pltpu.get_barrier_semaphore()
    for offset in range(1, n_f):
        pl.semaphore_signal(barrier, inc=1, device_id=to_f(peer_f(offset)), device_id_type=MESH)
    for offset in range(1, chips):
        pl.semaphore_signal(
            barrier, inc=1, device_id=to_r(peer_chip(offset) * 2 + core), device_id_type=MESH
        )
    pl.semaphore_signal(barrier, inc=1, device_id=to_r(mate), device_id_type=MESH)
    pl.semaphore_wait(barrier, n_f + chips - 1)

    def act_copy(offset, j):
        target = peer_f(offset)
        start = pl.multiple_of(target * cols + j * chunk, chunk)
        return pltpu.make_async_remote_copy(
            src_ref=act.at[0, :, pl.ds(start, chunk)],
            dst_ref=x_all.at[tok_block(me_f), chunk_cols(j)],
            send_sem=act_send.at[offset - 1, j],
            recv_sem=act_recv.at[offset - 1, j],
            device_id=to_f(target),
            device_id_type=MESH,
        )

    def act_arrival(offset, j):
        source = peer_f(-offset)
        return pltpu.make_async_remote_copy(
            src_ref=act.at[0, :, chunk_cols(j)],
            dst_ref=x_all.at[tok_block(source), chunk_cols(j)],
            send_sem=act_send.at[offset - 1, j],
            recv_sem=act_recv.at[offset - 1, j],
            device_id=to_f(source),
            device_id_type=MESH,
        )

    offsets = sorted(range(1, n_f), key=lambda o: (abs(o - n_f / 2), o))

    def send_chunk(j):
        for offset in offsets:
            act_copy(offset, j).start()

    send_chunk(0)

    def pair_copy(c):
        return pltpu.make_async_remote_copy(
            src_ref=weight.at[0, row_block(2 * c + 1 - core), :],
            dst_ref=pair_in.at[c],
            send_sem=pair_send.at[c],
            recv_sem=pair_recv.at[c],
            device_id=to_r(mate),
            device_id_type=MESH,
        )

    for c in range(chips):
        pair_copy(c).start()

    loads[0].wait()
    loads[1].wait()

    def norm_rows(i, carry):
        at = pl.ds(pl.multiple_of(i * 16, 16), 16)
        total = jnp.zeros((16, 1), F32)
        for piece in range(width // 1024):
            x = x_own[at, piece * 1024 : (piece + 1) * 1024].astype(F32)
            total += jnp.sum(x * x, axis=1, keepdims=True)
        scale = lax.rsqrt(total / width + NORM_EPS)
        k_scaled[at, :] = k_own[at, :].astype(F32) * scale
        return carry

    lax.fori_loop(0, tokens // 16, norm_rows, 0)
    k_all[:, tok_block(me_f)] = k_scaled[...].T.astype(BF16)

    def key_copy(offset, owner, target):
        return pltpu.make_async_remote_copy(
            src_ref=k_all.at[:, tok_block(owner)],
            dst_ref=k_all.at[:, tok_block(owner)],
            send_sem=k_send.at[offset - 1],
            recv_sem=k_recv.at[offset - 1],
            device_id=to_f(target),
            device_id_type=MESH,
        )

    for offset in offsets:
        key_copy(offset, me_f, peer_f(offset)).start()
    lax.fori_loop(1, chunks, lambda j, carry: (send_chunk(j), carry)[1], 0)

    def rs_copy(offset):
        target = peer_chip(offset)
        return pltpu.make_async_remote_copy(
            src_ref=pair_sum.at[target],
            dst_ref=rs_in.at[chip],
            send_sem=rs_send.at[offset - 1],
            recv_sem=rs_recv.at[offset - 1],
            device_id=to_r(target * 2 + core),
            device_id_type=MESH,
        )

    def rs_arrival(offset):
        source = peer_chip(-offset)
        return pltpu.make_async_remote_copy(
            src_ref=pair_sum.at[source],
            dst_ref=rs_in.at[source],
            send_sem=rs_send.at[offset - 1],
            recv_sem=rs_recv.at[offset - 1],
            device_id=to_r(source * 2 + core),
            device_id_type=MESH,
        )

    loads[2].wait()
    for c in range(chips):
        pair_copy(c).wait_recv()

    for offset in list(range(1, chips)) + [0]:
        target = peer_chip(offset)

        def add_rows(i, carry, target=target):
            at = pl.ds(pl.multiple_of(i * 16, 16), 16)
            own = pl.ds(pl.multiple_of((2 * target + core) * rows + i * 16, 16), 16)
            pair_sum[target, at, :] = (
                w_buf[own, :].astype(F32) + pair_in[target, at, :].astype(F32)
            ).astype(BF16)
            return carry

        lax.fori_loop(0, rows // 16, add_rows, 0)
        if offset:
            rs_copy(offset).start()

    loads[3].wait()
    loads[4].wait()
    for offset in range(1, chips):
        rs_arrival(offset).wait_recv()

    def outer_rows(i, carry):
        at = pl.ds(pl.multiple_of(i * 16, 16), 16)
        own = pl.ds(pl.multiple_of(me_r * rows + i * 16, 16), 16)
        piece = min(512, cols)
        for p in range(cols // piece):
            cs = slice(p * piece, (p + 1) * piece)
            total = pair_sum[chip, at, cs].astype(F32)
            for offset in range(1, chips):
                total += rs_in[peer_chip(offset), at, cs].astype(F32)
            params = outer_buf[at, cs]
            change = params - total / n_r
            mom = OUTER_MOMENTUM * mom_buf[at, cs] + change
            new = params - OUTER_RATE * (change + OUTER_MOMENTUM * mom)
            mom_new[at, cs] = mom
            outer_new[at, cs] = new
            par_all[own, cs] = new.astype(BF16)
        return carry

    lax.fori_loop(0, rows // 16, outer_rows, 0)

    def ag_copy(offset, owner, target):
        return pltpu.make_async_remote_copy(
            src_ref=par_all.at[row_block(owner), :],
            dst_ref=par_all.at[row_block(owner), :],
            send_sem=ag_send.at[offset - 1],
            recv_sem=ag_recv.at[offset - 1],
            device_id=to_r(target),
            device_id_type=MESH,
        )

    def fw_copy(offset, owner):
        return pltpu.make_async_remote_copy(
            src_ref=par_all.at[row_block(owner), :],
            dst_ref=par_all.at[row_block(owner), :],
            send_sem=fw_send.at[offset],
            recv_sem=fw_recv.at[offset],
            device_id=to_r(mate),
            device_id_type=MESH,
        )

    for offset in range(1, chips):
        ag_copy(offset, me_r, peer_chip(offset) * 2 + core).start()
    fw_copy(0, me_r).start()
    outs = [
        pltpu.make_async_copy(outer_new, outer_out, out_sem.at[0]),
        pltpu.make_async_copy(mom_new, momentum_out, out_sem.at[1]),
    ]
    for out in outs:
        out.start()
    for offset in range(1, chips):
        owner = peer_chip(-offset) * 2 + core
        ag_copy(offset, owner, owner).wait_recv()
        fw_copy(offset, owner).start()

    for load in loads[5:]:
        load.wait()
    for offset in offsets:
        source = peer_f(-offset)
        key_copy(offset, source, source).wait_recv()
    for offset in range(chips):
        fw_copy(offset, peer_chip(-offset) * 2 + 1 - core).wait_recv()

    step_value = jnp.full((1, chunk), step_ref[0], jnp.int32).astype(F32)
    inv_first = 1.0 / (1.0 - jnp.exp(step_value * math.log(BETA_ONE)))
    inv_second = 1.0 / (1.0 - jnp.exp(step_value * math.log(BETA_TWO)))
    tile = 32

    def merged_copy(j):
        return pltpu.make_async_copy(
            merged.at[:, chunk_cols(j)], merged_out.at[0, :, chunk_cols(j)], out_sem.at[5 + j]
        )

    def do_chunk(j, carry):
        for offset in offsets:
            act_arrival(offset, j).wait_recv()
        cs = chunk_cols(j)
        g_buf[...] = jnp.dot(k_all[...], x_all[:, cs], preferred_element_type=F32)
        gain_cols = gains[0, :, cs]
        scale = gain_cols * factor

        def do_rows(i, total):
            at = pl.ds(pl.multiple_of(i * tile, tile), tile)
            g = g_buf[at, :]
            w = w_buf[at, cs].astype(F32)
            prod = g * w
            for s in range(tile // 8):
                total += prod[s * 8 : (s + 1) * 8, :]
            grad = g * scale
            m = BETA_ONE * m_buf[at, cs].astype(F32) + (1.0 - BETA_ONE) * grad
            v = BETA_TWO * v_buf[at, cs].astype(F32) + (1.0 - BETA_TWO) * grad * grad
            update = (m * inv_first) / (jnp.sqrt(v * inv_second) + ADAM_EPS) + WEIGHT_DECAY * w
            local = w - INNER_RATE * update
            new = MIX_LOCAL * local + (1.0 - MIX_LOCAL) * par_all[at, cs].astype(F32)
            merged[at, cs] = new.astype(BF16)
            return total

        total = lax.fori_loop(0, features // tile, do_rows, jnp.zeros((8, chunk), F32))
        merged_copy(j).start()
        grad = jnp.sum(total, axis=0, keepdims=True) * factor
        m = BETA_ONE * gains[1, :, cs] + (1.0 - BETA_ONE) * grad
        v = BETA_TWO * gains[2, :, cs] + (1.0 - BETA_TWO) * grad * grad
        gains_new[0, :, cs] = gain_cols - INNER_RATE * (
            (m * inv_first) / (jnp.sqrt(v * inv_second) + ADAM_EPS)
        )
        gains_new[1, :, cs] = m
        gains_new[2, :, cs] = v
        return carry

    lax.fori_loop(0, chunks, do_chunk, 0)

    gain_outs = [
        pltpu.make_async_copy(gains_new.at[0], gain_out, out_sem.at[2]),
        pltpu.make_async_copy(gains_new.at[1], gfirst_out, out_sem.at[3]),
        pltpu.make_async_copy(gains_new.at[2], gsecond_out, out_sem.at[4]),
    ]
    for out in gain_outs:
        out.start()

    for offset in offsets:
        key_copy(offset, me_f, peer_f(offset)).wait_send()

    def drain(j, carry):
        for offset in offsets:
            act_copy(offset, j).wait_send()
        merged_copy(j).wait()
        return carry

    for c in range(chips):
        pair_copy(c).wait_send()
        fw_copy(c, me_r).wait_send()
    for offset in range(1, chips):
        rs_copy(offset).wait_send()
        ag_copy(offset, me_r, peer_chip(offset) * 2 + core).wait_send()
    lax.fori_loop(0, chunks, drain, 0)
    for out in outs + gain_outs:
        out.wait()


def shards(
    n_f,
    n_r,
    activations,
    key_grad,
    inner_weight,
    weight_first,
    weight_second,
    norm_gain,
    gain_first,
    gain_second,
    step_count,
    outer_params,
    outer_momentum,
):
    tokens, width = activations.shape[1:]
    features, cols = inner_weight.shape[1:]
    rows = outer_params.shape[0]
    chips = n_r // 2
    chunk = min(256, cols)
    chunks = cols // chunk
    dma = pltpu.SemaphoreType.DMA
    any_spec = pl.BlockSpec(memory_space=pl.ANY)
    return pl.pallas_call(
        functools.partial(kernel, n_f, n_r, chunk),
        out_shape=(
            jax.ShapeDtypeStruct(inner_weight.shape, BF16),
            jax.ShapeDtypeStruct(outer_params.shape, F32),
            jax.ShapeDtypeStruct(outer_params.shape, F32),
            jax.ShapeDtypeStruct(norm_gain.shape, F32),
            jax.ShapeDtypeStruct(norm_gain.shape, F32),
            jax.ShapeDtypeStruct(norm_gain.shape, F32),
        ),
        in_specs=[pl.BlockSpec(memory_space=pltpu.SMEM)] + [any_spec] * 10,
        out_specs=(any_spec,) * 6,
        scratch_shapes=[
            pltpu.VMEM((tokens, width), BF16),
            pltpu.VMEM((n_f * tokens, cols), BF16),
            pltpu.VMEM((tokens, features), BF16),
            pltpu.VMEM((tokens, features), F32),
            pltpu.VMEM((features, n_f * tokens), BF16),
            pltpu.VMEM((features, cols), BF16),
            pltpu.VMEM((features, cols), BF16),
            pltpu.VMEM((features, cols), BF16),
            pltpu.VMEM((features, chunk), F32),
            pltpu.VMEM((features, cols), BF16),
            pltpu.VMEM((chips, rows, cols), BF16),
            pltpu.VMEM((chips, rows, cols), BF16),
            pltpu.VMEM((chips, rows, cols), BF16),
            pltpu.VMEM((features, cols), BF16),
            pltpu.VMEM((rows, cols), F32),
            pltpu.VMEM((rows, cols), F32),
            pltpu.VMEM((rows, cols), F32),
            pltpu.VMEM((rows, cols), F32),
            pltpu.VMEM((3, 1, cols), F32),
            pltpu.VMEM((3, 1, cols), F32),
            dma((11,)),
            dma((5 + chunks,)),
            dma((n_f - 1, chunks)),
            dma((n_f - 1, chunks)),
            dma((n_f - 1,)),
            dma((n_f - 1,)),
            dma((chips,)),
            dma((chips,)),
            dma((chips - 1,)),
            dma((chips - 1,)),
            dma((chips - 1,)),
            dma((chips - 1,)),
            dma((chips,)),
            dma((chips,)),
        ],
        compiler_params=pltpu.CompilerParams(
            collective_id=0, has_side_effects=True, vmem_limit_bytes=48 * 1024 * 1024
        ),
        name="diloco_step",
    )(
        step_count.reshape(1),
        activations,
        key_grad,
        inner_weight,
        weight_first,
        weight_second,
        norm_gain,
        gain_first,
        gain_second,
        outer_params,
        outer_momentum,
    )


def solution(mesh):
    return jax.shard_map(
        functools.partial(shards, mesh.shape["fsdp"], mesh.shape["replica"]),
        mesh=mesh,
        in_specs=(
            P("replica", "fsdp", None),
            P("replica", "fsdp", None),
            P("replica", None, "fsdp"),
            P("replica", None, "fsdp"),
            P("replica", None, "fsdp"),
            P("replica", "fsdp"),
            P("replica", "fsdp"),
            P("replica", "fsdp"),
            P(),
            P("replica", "fsdp"),
            P("replica", "fsdp"),
        ),
        out_specs=(
            P("replica", None, "fsdp"),
            P("replica", "fsdp"),
            P("replica", "fsdp"),
            P("replica", "fsdp"),
            P("replica", "fsdp"),
            P("replica", "fsdp"),
        ),
        check_vma=False,
    )
```

```python
import functools
import math

import jax
import jax.numpy as jnp
from jax import lax
from jax.experimental import pallas as pl
from jax.experimental.pallas import tpu as pltpu
from jax.sharding import PartitionSpec as P

BETA_ONE = 0.9
BETA_TWO = 0.95
ADAM_EPS = 1e-08
INNER_RATE = 0.25
WEIGHT_DECAY = 0.1
OUTER_RATE = 0.7
OUTER_MOMENTUM = 0.9
MIX_LOCAL = 0.5
NORM_EPS = 1e-05

MESH = pl.DeviceIdType.MESH
F32 = jnp.float32
BF16 = jnp.bfloat16
VMEM_LIMIT = 60 * 1024 * 1024


def kernel(
    n_f,
    n_r,
    chunk,
    step_ref,
    act,
    key,
    weight,
    first,
    second,
    gain,
    gfirst,
    gsecond,
    outer,
    momentum,
    merged_out,
    outer_out,
    momentum_out,
    gain_out,
    gfirst_out,
    gsecond_out,
    x_own,
    x_all,
    k_own,
    k_scaled,
    k_all,
    w_buf,
    m_buf,
    v_buf,
    g_buf,
    merged,
    pair_in,
    pair_sum,
    rs_in,
    par_all,
    outer_buf,
    mom_buf,
    outer_new,
    mom_new,
    gains,
    gains_new,
    local_sem,
    out_sem,
    act_send,
    act_recv,
    k_send,
    k_recv,
    pair_send,
    pair_recv,
    rs_send,
    rs_recv,
    ag_send,
    ag_recv,
    fw_send,
    fw_recv,
):
    tokens = act.shape[1]
    width = act.shape[2]
    cols = weight.shape[2]
    features = weight.shape[1]
    rows = outer.shape[0]
    chunks = cols // chunk
    chips = n_r // 2
    factor = width ** (-0.5)
    early = min(2, chunks)

    me_f = lax.axis_index("fsdp")
    me_r = lax.axis_index("replica")
    chip, core = me_r // 2, me_r % 2
    mate = chip * 2 + 1 - core

    def peer_f(offset):
        return lax.rem(me_f + offset + n_f, n_f)

    def peer_chip(offset):
        return lax.rem(chip + offset + chips, chips)

    def to_f(index):
        return (me_r, index)

    def to_r(index):
        return (index, me_f)

    def row_block(index):
        return pl.ds(pl.multiple_of(index * rows, rows), rows)

    def tok_block(index):
        return pl.ds(pl.multiple_of(index * tokens, tokens), tokens)

    def chunk_cols(j):
        return pl.ds(pl.multiple_of(j * chunk, chunk), chunk)

    loads = [
        pltpu.make_async_copy(act.at[0], x_own, local_sem.at[0]),
        pltpu.make_async_copy(key.at[0], k_own, local_sem.at[1]),
        pltpu.make_async_copy(weight.at[0], w_buf, local_sem.at[2]),
        pltpu.make_async_copy(outer, outer_buf, local_sem.at[3]),
        pltpu.make_async_copy(momentum, mom_buf, local_sem.at[4]),
        pltpu.make_async_copy(
            act.at[0, :, pl.ds(pl.multiple_of(me_f * cols, cols), cols)],
            x_all.at[tok_block(me_f), :],
            local_sem.at[5],
        ),
        pltpu.make_async_copy(first.at[0], m_buf, local_sem.at[6]),
        pltpu.make_async_copy(second.at[0], v_buf, local_sem.at[7]),
        pltpu.make_async_copy(gain, gains.at[0], local_sem.at[8]),
        pltpu.make_async_copy(gfirst, gains.at[1], local_sem.at[9]),
        pltpu.make_async_copy(gsecond, gains.at[2], local_sem.at[10]),
    ]

    barrier = pltpu.get_barrier_semaphore()
    for offset in range(1, n_f):
        pl.semaphore_signal(barrier, inc=1, device_id=to_f(peer_f(offset)), device_id_type=MESH)
    for offset in range(1, chips):
        pl.semaphore_signal(
            barrier, inc=1, device_id=to_r(peer_chip(offset) * 2 + core), device_id_type=MESH
        )
    pl.semaphore_signal(barrier, inc=1, device_id=to_r(mate), device_id_type=MESH)
    for load in loads:
        load.start()
    pl.semaphore_wait(barrier, n_f + chips - 1)

    def act_copy(offset, j):
        target = peer_f(offset)
        start = pl.multiple_of(target * cols + j * chunk, chunk)
        return pltpu.make_async_remote_copy(
            src_ref=act.at[0, :, pl.ds(start, chunk)],
            dst_ref=x_all.at[tok_block(me_f), chunk_cols(j)],
            send_sem=act_send.at[offset - 1, j],
            recv_sem=act_recv.at[offset - 1, j],
            device_id=to_f(target),
            device_id_type=MESH,
        )

    def act_arrival(offset, j):
        source = peer_f(-offset)
        return pltpu.make_async_remote_copy(
            src_ref=act.at[0, :, chunk_cols(j)],
            dst_ref=x_all.at[tok_block(source), chunk_cols(j)],
            send_sem=act_send.at[offset - 1, j],
            recv_sem=act_recv.at[offset - 1, j],
            device_id=to_f(source),
            device_id_type=MESH,
        )

    offsets = sorted(range(1, n_f), key=lambda o: (abs(o - n_f / 2), o))

    def send_chunk(j):
        for offset in offsets:
            act_copy(offset, j).start()

    send_chunk(0)

    def pair_copy(c):
        return pltpu.make_async_remote_copy(
            src_ref=weight.at[0, row_block(2 * c + 1 - core), :],
            dst_ref=pair_in.at[c],
            send_sem=pair_send.at[c],
            recv_sem=pair_recv.at[c],
            device_id=to_r(mate),
            device_id_type=MESH,
        )

    for c in range(chips):
        pair_copy(c).start()

    loads[0].wait()
    loads[1].wait()

    def norm_rows(i, carry):
        at = pl.ds(pl.multiple_of(i * 16, 16), 16)
        total = jnp.zeros((16, 1), F32)
        for piece in range(width // 1024):
            x = x_own[at, piece * 1024 : (piece + 1) * 1024].astype(F32)
            total += jnp.sum(x * x, axis=1, keepdims=True)
        scale = lax.rsqrt(total / width + NORM_EPS)
        k_scaled[at, :] = k_own[at, :].astype(F32) * scale
        return carry

    lax.fori_loop(0, tokens // 16, norm_rows, 0)
    k_all[:, tok_block(me_f)] = k_scaled[...].T.astype(BF16)

    def key_copy(owner, step):
        return pltpu.make_async_remote_copy(
            src_ref=k_all.at[:, tok_block(owner)],
            dst_ref=k_all.at[:, tok_block(owner)],
            send_sem=k_send.at[(step + 1) // 2, owner],
            recv_sem=k_recv.at[owner],
            device_id=to_f(peer_f(step)),
            device_id_type=MESH,
        )

    @pl.when(me_f < n_f - 1)
    def _():
        key_copy(me_f, 1).start()

    @pl.when(me_f > 0)
    def _():
        key_copy(me_f, -1).start()

    lax.fori_loop(1, early, lambda j, carry: (send_chunk(j), carry)[1], 0)

    def pass_keys(distance):
        @pl.when(me_f >= distance)
        def _():
            key_copy(me_f - distance, 1).wait_recv()

            @pl.when(me_f < n_f - 1)
            def _():
                key_copy(me_f - distance, 1).start()

        @pl.when(me_f + distance < n_f)
        def _():
            key_copy(me_f + distance, -1).wait_recv()

            @pl.when(me_f > 0)
            def _():
                key_copy(me_f + distance, -1).start()

    def rs_copy(offset):
        target = peer_chip(offset)
        return pltpu.make_async_remote_copy(
            src_ref=pair_sum.at[target],
            dst_ref=rs_in.at[chip],
            send_sem=rs_send.at[offset - 1],
            recv_sem=rs_recv.at[offset - 1],
            device_id=to_r(target * 2 + core),
            device_id_type=MESH,
        )

    def rs_arrival(offset):
        source = peer_chip(-offset)
        return pltpu.make_async_remote_copy(
            src_ref=pair_sum.at[source],
            dst_ref=rs_in.at[source],
            send_sem=rs_send.at[offset - 1],
            recv_sem=rs_recv.at[offset - 1],
            device_id=to_r(source * 2 + core),
            device_id_type=MESH,
        )

    loads[2].wait()
    for c in range(chips):
        pair_copy(c).wait_recv()

    for offset in list(range(1, chips)) + [0]:
        target = peer_chip(offset)

        def add_rows(i, carry, target=target):
            at = pl.ds(pl.multiple_of(i * 16, 16), 16)
            own = pl.ds(pl.multiple_of((2 * target + core) * rows + i * 16, 16), 16)
            pair_sum[target, at, :] = (
                w_buf[own, :].astype(F32) + pair_in[target, at, :].astype(F32)
            ).astype(BF16)
            return carry

        lax.fori_loop(0, rows // 16, add_rows, 0)
        if offset:
            rs_copy(offset).start()

    for distance in range(1, n_f - 1):
        pass_keys(distance)
    lax.fori_loop(early, chunks, lambda j, carry: (send_chunk(j), carry)[1], 0)

    loads[3].wait()
    loads[4].wait()
    for offset in range(1, chips):
        rs_arrival(offset).wait_recv()

    def outer_rows(i, carry):
        at = pl.ds(pl.multiple_of(i * 16, 16), 16)
        own = pl.ds(pl.multiple_of(me_r * rows + i * 16, 16), 16)
        piece = min(512, cols)
        for p in range(cols // piece):
            cs = slice(p * piece, (p + 1) * piece)
            total = pair_sum[chip, at, cs].astype(F32)
            for offset in range(1, chips):
                total += rs_in[peer_chip(offset), at, cs].astype(F32)
            params = outer_buf[at, cs]
            change = params - total / n_r
            mom = OUTER_MOMENTUM * mom_buf[at, cs] + change
            new = params - OUTER_RATE * (change + OUTER_MOMENTUM * mom)
            mom_new[at, cs] = mom
            outer_new[at, cs] = new
            par_all[own, cs] = new.astype(BF16)
        return carry

    lax.fori_loop(0, rows // 16, outer_rows, 0)

    def ag_copy(offset, owner, target):
        return pltpu.make_async_remote_copy(
            src_ref=par_all.at[row_block(owner), :],
            dst_ref=par_all.at[row_block(owner), :],
            send_sem=ag_send.at[offset - 1],
            recv_sem=ag_recv.at[offset - 1],
            device_id=to_r(target),
            device_id_type=MESH,
        )

    def fw_copy(offset, owner):
        return pltpu.make_async_remote_copy(
            src_ref=par_all.at[row_block(owner), :],
            dst_ref=par_all.at[row_block(owner), :],
            send_sem=fw_send.at[offset],
            recv_sem=fw_recv.at[offset],
            device_id=to_r(mate),
            device_id_type=MESH,
        )

    for offset in range(1, chips):
        ag_copy(offset, me_r, peer_chip(offset) * 2 + core).start()
    fw_copy(0, me_r).start()
    outs = [
        pltpu.make_async_copy(outer_new, outer_out, out_sem.at[0]),
        pltpu.make_async_copy(mom_new, momentum_out, out_sem.at[1]),
    ]
    for out in outs:
        out.start()
    for offset in range(1, chips):
        owner = peer_chip(-offset) * 2 + core
        ag_copy(offset, owner, owner).wait_recv()
        fw_copy(offset, owner).start()

    for load in loads[5:]:
        load.wait()
    pass_keys(n_f - 1)
    for offset in range(chips):
        fw_copy(offset, peer_chip(-offset) * 2 + 1 - core).wait_recv()

    step_value = jnp.full((1, chunk), step_ref[0], jnp.int32).astype(F32)
    inv_first = 1.0 / (1.0 - jnp.exp(step_value * math.log(BETA_ONE)))
    inv_second = 1.0 / (1.0 - jnp.exp(step_value * math.log(BETA_TWO)))
    tile = 32

    def merged_copy(j):
        return pltpu.make_async_copy(
            merged.at[:, chunk_cols(j)], merged_out.at[0, :, chunk_cols(j)], out_sem.at[5 + j]
        )

    def do_chunk(j, carry):
        for offset in offsets:
            act_arrival(offset, j).wait_recv()
        cs = chunk_cols(j)
        g_buf[...] = jnp.dot(k_all[...], x_all[:, cs], preferred_element_type=F32)
        gain_cols = gains[0, :, cs]
        scale = gain_cols * factor

        def do_rows(i, total):
            at = pl.ds(pl.multiple_of(i * tile, tile), tile)
            g = g_buf[at, :]
            w = w_buf[at, cs].astype(F32)
            prod = g * w
            for s in range(tile // 8):
                total += prod[s * 8 : (s + 1) * 8, :]
            grad = g * scale
            m = BETA_ONE * m_buf[at, cs].astype(F32) + (1.0 - BETA_ONE) * grad
            v = BETA_TWO * v_buf[at, cs].astype(F32) + (1.0 - BETA_TWO) * grad * grad
            update = (m * inv_first) / (jnp.sqrt(v * inv_second) + ADAM_EPS) + WEIGHT_DECAY * w
            local = w - INNER_RATE * update
            new = MIX_LOCAL * local + (1.0 - MIX_LOCAL) * par_all[at, cs].astype(F32)
            merged[at, cs] = new.astype(BF16)
            return total

        total = lax.fori_loop(0, features // tile, do_rows, jnp.zeros((8, chunk), F32))
        merged_copy(j).start()
        grad = jnp.sum(total, axis=0, keepdims=True) * factor
        m = BETA_ONE * gains[1, :, cs] + (1.0 - BETA_ONE) * grad
        v = BETA_TWO * gains[2, :, cs] + (1.0 - BETA_TWO) * grad * grad
        gains_new[0, :, cs] = gain_cols - INNER_RATE * (
            (m * inv_first) / (jnp.sqrt(v * inv_second) + ADAM_EPS)
        )
        gains_new[1, :, cs] = m
        gains_new[2, :, cs] = v
        return carry

    lax.fori_loop(0, chunks, do_chunk, 0)

    gain_outs = [
        pltpu.make_async_copy(gains_new.at[0], gain_out, out_sem.at[2]),
        pltpu.make_async_copy(gains_new.at[1], gfirst_out, out_sem.at[3]),
        pltpu.make_async_copy(gains_new.at[2], gsecond_out, out_sem.at[4]),
    ]
    for out in gain_outs:
        out.start()

    for owner in range(n_f):

        @pl.when(jnp.logical_and(me_f >= owner, me_f < n_f - 1))
        def _(owner=owner):
            key_copy(owner, 1).wait_send()

        @pl.when(jnp.logical_and(me_f <= owner, me_f > 0))
        def _(owner=owner):
            key_copy(owner, -1).wait_send()


    def drain(j, carry):
        for offset in offsets:
            act_copy(offset, j).wait_send()
        merged_copy(j).wait()
        return carry

    for c in range(chips):
        pair_copy(c).wait_send()
        fw_copy(c, me_r).wait_send()
    for offset in range(1, chips):
        rs_copy(offset).wait_send()
        ag_copy(offset, me_r, peer_chip(offset) * 2 + core).wait_send()
    lax.fori_loop(0, chunks, drain, 0)
    for out in outs + gain_outs:
        out.wait()


def hand_over(*refs):
    sem = refs[-1]
    copies = [
        pltpu.make_async_copy(refs[i], refs[6 + i], sem.at[i]) for i in range(6)
    ]
    for copy in copies:
        copy.start()
    for copy in copies:
        copy.wait()


def shards(
    n_f,
    n_r,
    activations,
    key_grad,
    inner_weight,
    weight_first,
    weight_second,
    norm_gain,
    gain_first,
    gain_second,
    step_count,
    outer_params,
    outer_momentum,
):
    tokens, width = activations.shape[1:]
    features, cols = inner_weight.shape[1:]
    rows = outer_params.shape[0]
    chips = n_r // 2
    chunk = min(256, cols)
    chunks = cols // chunk
    dma = pltpu.SemaphoreType.DMA
    any_spec = pl.BlockSpec(memory_space=pl.ANY)
    results = pl.pallas_call(
        functools.partial(kernel, n_f, n_r, chunk),
        out_shape=(
            jax.ShapeDtypeStruct(inner_weight.shape, BF16),
            jax.ShapeDtypeStruct(outer_params.shape, F32),
            jax.ShapeDtypeStruct(outer_params.shape, F32),
            jax.ShapeDtypeStruct(norm_gain.shape, F32),
            jax.ShapeDtypeStruct(norm_gain.shape, F32),
            jax.ShapeDtypeStruct(norm_gain.shape, F32),
        ),
        in_specs=[pl.BlockSpec(memory_space=pltpu.SMEM)] + [any_spec] * 10,
        out_specs=(any_spec,) * 6,
        scratch_shapes=[
            pltpu.VMEM((tokens, width), BF16),
            pltpu.VMEM((n_f * tokens, cols), BF16),
            pltpu.VMEM((tokens, features), BF16),
            pltpu.VMEM((tokens, features), F32),
            pltpu.VMEM((features, n_f * tokens), BF16),
            pltpu.VMEM((features, cols), BF16),
            pltpu.VMEM((features, cols), BF16),
            pltpu.VMEM((features, cols), BF16),
            pltpu.VMEM((features, chunk), F32),
            pltpu.VMEM((features, cols), BF16),
            pltpu.VMEM((chips, rows, cols), BF16),
            pltpu.VMEM((chips, rows, cols), BF16),
            pltpu.VMEM((chips, rows, cols), BF16),
            pltpu.VMEM((features, cols), BF16),
            pltpu.VMEM((rows, cols), F32),
            pltpu.VMEM((rows, cols), F32),
            pltpu.VMEM((rows, cols), F32),
            pltpu.VMEM((rows, cols), F32),
            pltpu.VMEM((3, 1, cols), F32),
            pltpu.VMEM((3, 1, cols), F32),
            dma((11,)),
            dma((5 + chunks,)),
            dma((n_f - 1, chunks)),
            dma((n_f - 1, chunks)),
            dma((2, n_f)),
            dma((n_f,)),
            dma((chips,)),
            dma((chips,)),
            dma((chips - 1,)),
            dma((chips - 1,)),
            dma((chips - 1,)),
            dma((chips - 1,)),
            dma((chips,)),
            dma((chips,)),
        ],
        compiler_params=pltpu.CompilerParams(
            collective_id=0, has_side_effects=True, vmem_limit_bytes=VMEM_LIMIT
        ),
        name="diloco_step",
    )(
        step_count.reshape(1),
        activations,
        key_grad,
        inner_weight,
        weight_first,
        weight_second,
        norm_gain,
        gain_first,
        gain_second,
        outer_params,
        outer_momentum,
    )
    return pl.pallas_call(
        hand_over,
        out_shape=tuple(jax.ShapeDtypeStruct(r.shape, r.dtype) for r in results),
        in_specs=[pl.BlockSpec(memory_space=pltpu.VMEM)] * 6,
        out_specs=(any_spec,) * 6,
        scratch_shapes=[dma((6,))],
        name="hand_over",
    )(*results)


def solution(mesh):
    return jax.shard_map(
        functools.partial(shards, mesh.shape["fsdp"], mesh.shape["replica"]),
        mesh=mesh,
        in_specs=(
            P("replica", "fsdp", None),
            P("replica", "fsdp", None),
            P("replica", None, "fsdp"),
            P("replica", None, "fsdp"),
            P("replica", None, "fsdp"),
            P("replica", "fsdp"),
            P("replica", "fsdp"),
            P("replica", "fsdp"),
            P(),
            P("replica", "fsdp"),
            P("replica", "fsdp"),
        ),
        out_specs=(
            P("replica", None, "fsdp"),
            P("replica", "fsdp"),
            P("replica", "fsdp"),
            P("replica", "fsdp"),
            P("replica", "fsdp"),
            P("replica", "fsdp"),
        ),
        check_vma=False,
    )
```

```python
import functools
import math

import jax
import jax.numpy as jnp
from jax import lax
from jax.experimental import pallas as pl
from jax.experimental.pallas import tpu as pltpu
from jax.sharding import PartitionSpec as P

BETA_ONE = 0.9
BETA_TWO = 0.95
ADAM_EPS = 1e-08
INNER_RATE = 0.25
WEIGHT_DECAY = 0.1
OUTER_RATE = 0.7
OUTER_MOMENTUM = 0.9
MIX_LOCAL = 0.5
NORM_EPS = 1e-05

MESH = pl.DeviceIdType.MESH
F32 = jnp.float32
BF16 = jnp.bfloat16
VMEM_LIMIT = 60 * 1024 * 1024


def kernel(
    n_f,
    n_r,
    chunk,
    step_ref,
    act,
    key,
    weight,
    first,
    second,
    gain,
    gfirst,
    gsecond,
    outer,
    momentum,
    merged_out,
    outer_out,
    momentum_out,
    gain_out,
    gfirst_out,
    gsecond_out,
    x_own,
    x_all,
    k_own,
    k_scaled,
    k_all,
    w_buf,
    m_buf,
    v_buf,
    g_buf,
    merged,
    pair_in,
    pair_sum,
    rs_in,
    par_all,
    outer_buf,
    mom_buf,
    outer_new,
    mom_new,
    gains,
    gains_new,
    local_sem,
    out_sem,
    act_send,
    act_recv,
    k_send,
    k_recv,
    pair_send,
    pair_recv,
    rs_send,
    rs_recv,
    ag_send,
    ag_recv,
    fw_send,
    fw_recv,
):
    tokens = act.shape[1]
    width = act.shape[2]
    cols = weight.shape[2]
    features = weight.shape[1]
    rows = outer.shape[0]
    chunks = cols // chunk
    chips = n_r // 2
    factor = width ** (-0.5)
    early = min(2, chunks)
    later = min(3, chunks)

    me_f = lax.axis_index("fsdp")
    me_r = lax.axis_index("replica")
    chip, core = me_r // 2, me_r % 2
    mate = chip * 2 + 1 - core

    def peer_f(offset):
        return lax.rem(me_f + offset + n_f, n_f)

    def peer_chip(offset):
        return lax.rem(chip + offset + chips, chips)

    def to_f(index):
        return (me_r, index)

    def to_r(index):
        return (index, me_f)

    def row_block(index):
        return pl.ds(pl.multiple_of(index * rows, rows), rows)

    def tok_block(index):
        return pl.ds(pl.multiple_of(index * tokens, tokens), tokens)

    def chunk_cols(j):
        return pl.ds(pl.multiple_of(j * chunk, chunk), chunk)

    loads = [
        pltpu.make_async_copy(act.at[0], x_own, local_sem.at[0]),
        pltpu.make_async_copy(key.at[0], k_own, local_sem.at[1]),
        pltpu.make_async_copy(weight.at[0], w_buf, local_sem.at[2]),
        pltpu.make_async_copy(outer, outer_buf, local_sem.at[3]),
        pltpu.make_async_copy(momentum, mom_buf, local_sem.at[4]),
        pltpu.make_async_copy(
            act.at[0, :, pl.ds(pl.multiple_of(me_f * cols, cols), cols)],
            x_all.at[tok_block(me_f), :],
            local_sem.at[5],
        ),
        pltpu.make_async_copy(first.at[0], m_buf, local_sem.at[6]),
        pltpu.make_async_copy(second.at[0], v_buf, local_sem.at[7]),
        pltpu.make_async_copy(gain, gains.at[0], local_sem.at[8]),
        pltpu.make_async_copy(gfirst, gains.at[1], local_sem.at[9]),
        pltpu.make_async_copy(gsecond, gains.at[2], local_sem.at[10]),
    ]

    barrier = pltpu.get_barrier_semaphore()
    for offset in range(1, n_f):
        pl.semaphore_signal(barrier, inc=1, device_id=to_f(peer_f(offset)), device_id_type=MESH)
    for offset in range(1, chips):
        pl.semaphore_signal(
            barrier, inc=1, device_id=to_r(peer_chip(offset) * 2 + core), device_id_type=MESH
        )
    pl.semaphore_signal(barrier, inc=1, device_id=to_r(mate), device_id_type=MESH)
    for load in loads:
        load.start()
    pl.semaphore_wait(barrier, n_f + chips - 1)

    def act_copy(offset, j):
        target = peer_f(offset)
        start = pl.multiple_of(target * cols + j * chunk, chunk)
        return pltpu.make_async_remote_copy(
            src_ref=act.at[0, :, pl.ds(start, chunk)],
            dst_ref=x_all.at[tok_block(me_f), chunk_cols(j)],
            send_sem=act_send.at[offset - 1, j],
            recv_sem=act_recv.at[offset - 1, j],
            device_id=to_f(target),
            device_id_type=MESH,
        )

    def act_arrival(offset, j):
        source = peer_f(-offset)
        return pltpu.make_async_remote_copy(
            src_ref=act.at[0, :, chunk_cols(j)],
            dst_ref=x_all.at[tok_block(source), chunk_cols(j)],
            send_sem=act_send.at[offset - 1, j],
            recv_sem=act_recv.at[offset - 1, j],
            device_id=to_f(source),
            device_id_type=MESH,
        )

    offsets = sorted(range(1, n_f), key=lambda o: (abs(o - n_f / 2), o))

    def send_chunk(j):
        for offset in offsets:
            act_copy(offset, j).start()

    send_chunk(0)

    def pair_copy(c):
        return pltpu.make_async_remote_copy(
            src_ref=weight.at[0, row_block(2 * c + 1 - core), :],
            dst_ref=pair_in.at[c],
            send_sem=pair_send.at[c],
            recv_sem=pair_recv.at[c],
            device_id=to_r(mate),
            device_id_type=MESH,
        )

    for c in range(chips):
        pair_copy(c).start()

    loads[0].wait()
    loads[1].wait()

    def norm_rows(i, carry):
        at = pl.ds(pl.multiple_of(i * 16, 16), 16)
        total = jnp.zeros((16, 1), F32)
        for piece in range(width // 1024):
            x = x_own[at, piece * 1024 : (piece + 1) * 1024].astype(F32)
            total += jnp.sum(x * x, axis=1, keepdims=True)
        scale = lax.rsqrt(total / width + NORM_EPS)
        k_scaled[at, :] = k_own[at, :].astype(F32) * scale
        return carry

    lax.fori_loop(0, tokens // 16, norm_rows, 0)
    k_all[:, tok_block(me_f)] = k_scaled[...].T.astype(BF16)

    def key_copy(owner, step):
        return pltpu.make_async_remote_copy(
            src_ref=k_all.at[:, tok_block(owner)],
            dst_ref=k_all.at[:, tok_block(owner)],
            send_sem=k_send.at[(step + 1) // 2, owner],
            recv_sem=k_recv.at[owner],
            device_id=to_f(peer_f(step)),
            device_id_type=MESH,
        )

    @pl.when(me_f < n_f - 1)
    def _():
        key_copy(me_f, 1).start()

    @pl.when(me_f > 0)
    def _():
        key_copy(me_f, -1).start()

    lax.fori_loop(1, early, lambda j, carry: (send_chunk(j), carry)[1], 0)

    def pass_keys(distance):
        @pl.when(me_f >= distance)
        def _():
            key_copy(me_f - distance, 1).wait_recv()

            @pl.when(me_f < n_f - 1)
            def _():
                key_copy(me_f - distance, 1).start()

        @pl.when(me_f + distance < n_f)
        def _():
            key_copy(me_f + distance, -1).wait_recv()

            @pl.when(me_f > 0)
            def _():
                key_copy(me_f + distance, -1).start()

    def rs_copy(offset):
        target = peer_chip(offset)
        return pltpu.make_async_remote_copy(
            src_ref=pair_sum.at[target],
            dst_ref=rs_in.at[chip],
            send_sem=rs_send.at[offset - 1],
            recv_sem=rs_recv.at[offset - 1],
            device_id=to_r(target * 2 + core),
            device_id_type=MESH,
        )

    def rs_arrival(offset):
        source = peer_chip(-offset)
        return pltpu.make_async_remote_copy(
            src_ref=pair_sum.at[source],
            dst_ref=rs_in.at[source],
            send_sem=rs_send.at[offset - 1],
            recv_sem=rs_recv.at[offset - 1],
            device_id=to_r(source * 2 + core),
            device_id_type=MESH,
        )

    loads[2].wait()
    for c in range(chips):
        pair_copy(c).wait_recv()

    for offset in list(range(1, chips)) + [0]:
        target = peer_chip(offset)

        def add_rows(i, carry, target=target):
            at = pl.ds(pl.multiple_of(i * 16, 16), 16)
            own = pl.ds(pl.multiple_of((2 * target + core) * rows + i * 16, 16), 16)
            pair_sum[target, at, :] = (
                w_buf[own, :].astype(F32) + pair_in[target, at, :].astype(F32)
            ).astype(BF16)
            return carry

        lax.fori_loop(0, rows // 16, add_rows, 0)
        if offset:
            rs_copy(offset).start()

    pass_keys(1)
    lax.fori_loop(early, later, lambda j, carry: (send_chunk(j), carry)[1], 0)
    for distance in range(2, n_f - 1):
        pass_keys(distance)
    lax.fori_loop(later, chunks, lambda j, carry: (send_chunk(j), carry)[1], 0)

    loads[3].wait()
    loads[4].wait()
    for offset in range(1, chips):
        rs_arrival(offset).wait_recv()

    def outer_rows(i, carry):
        at = pl.ds(pl.multiple_of(i * 16, 16), 16)
        own = pl.ds(pl.multiple_of(me_r * rows + i * 16, 16), 16)
        piece = min(512, cols)
        for p in range(cols // piece):
            cs = slice(p * piece, (p + 1) * piece)
            total = pair_sum[chip, at, cs].astype(F32)
            for offset in range(1, chips):
                total += rs_in[peer_chip(offset), at, cs].astype(F32)
            params = outer_buf[at, cs]
            change = params - total / n_r
            mom = OUTER_MOMENTUM * mom_buf[at, cs] + change
            new = params - OUTER_RATE * (change + OUTER_MOMENTUM * mom)
            mom_new[at, cs] = mom
            outer_new[at, cs] = new
            par_all[own, cs] = new.astype(BF16)
        return carry

    lax.fori_loop(0, rows // 16, outer_rows, 0)

    def ag_copy(offset, owner, target):
        return pltpu.make_async_remote_copy(
            src_ref=par_all.at[row_block(owner), :],
            dst_ref=par_all.at[row_block(owner), :],
            send_sem=ag_send.at[offset - 1],
            recv_sem=ag_recv.at[offset - 1],
            device_id=to_r(target),
            device_id_type=MESH,
        )

    def fw_copy(offset, owner):
        return pltpu.make_async_remote_copy(
            src_ref=par_all.at[row_block(owner), :],
            dst_ref=par_all.at[row_block(owner), :],
            send_sem=fw_send.at[offset],
            recv_sem=fw_recv.at[offset],
            device_id=to_r(mate),
            device_id_type=MESH,
        )

    for offset in range(1, chips):
        ag_copy(offset, me_r, peer_chip(offset) * 2 + core).start()
    fw_copy(0, me_r).start()
    outs = [
        pltpu.make_async_copy(outer_new, outer_out, out_sem.at[0]),
        pltpu.make_async_copy(mom_new, momentum_out, out_sem.at[1]),
    ]
    for out in outs:
        out.start()
    for offset in range(1, chips):
        owner = peer_chip(-offset) * 2 + core
        ag_copy(offset, owner, owner).wait_recv()
        fw_copy(offset, owner).start()

    for load in loads[5:]:
        load.wait()
    pass_keys(n_f - 1)
    for offset in range(chips):
        fw_copy(offset, peer_chip(-offset) * 2 + 1 - core).wait_recv()

    step_value = jnp.full((1, chunk), step_ref[0], jnp.int32).astype(F32)
    inv_first = 1.0 / (1.0 - jnp.exp(step_value * math.log(BETA_ONE)))
    inv_second = 1.0 / (1.0 - jnp.exp(step_value * math.log(BETA_TWO)))
    tile = 32

    def merged_copy(j):
        return pltpu.make_async_copy(
            merged.at[:, chunk_cols(j)], merged_out.at[0, :, chunk_cols(j)], out_sem.at[5 + j]
        )

    def do_chunk(j, carry):
        for offset in offsets:
            act_arrival(offset, j).wait_recv()
        cs = chunk_cols(j)
        g_buf[...] = jnp.dot(k_all[...], x_all[:, cs], preferred_element_type=F32)
        gain_cols = gains[0, :, cs]
        scale = gain_cols * factor

        def do_rows(i, total):
            at = pl.ds(pl.multiple_of(i * tile, tile), tile)
            g = g_buf[at, :]
            w = w_buf[at, cs].astype(F32)
            prod = g * w
            for s in range(tile // 8):
                total += prod[s * 8 : (s + 1) * 8, :]
            grad = g * scale
            m = BETA_ONE * m_buf[at, cs].astype(F32) + (1.0 - BETA_ONE) * grad
            v = BETA_TWO * v_buf[at, cs].astype(F32) + (1.0 - BETA_TWO) * grad * grad
            update = (m * inv_first) / (jnp.sqrt(v * inv_second) + ADAM_EPS) + WEIGHT_DECAY * w
            local = w - INNER_RATE * update
            new = MIX_LOCAL * local + (1.0 - MIX_LOCAL) * par_all[at, cs].astype(F32)
            merged[at, cs] = new.astype(BF16)
            return total

        total = lax.fori_loop(0, features // tile, do_rows, jnp.zeros((8, chunk), F32))
        merged_copy(j).start()
        grad = jnp.sum(total, axis=0, keepdims=True) * factor
        m = BETA_ONE * gains[1, :, cs] + (1.0 - BETA_ONE) * grad
        v = BETA_TWO * gains[2, :, cs] + (1.0 - BETA_TWO) * grad * grad
        gains_new[0, :, cs] = gain_cols - INNER_RATE * (
            (m * inv_first) / (jnp.sqrt(v * inv_second) + ADAM_EPS)
        )
        gains_new[1, :, cs] = m
        gains_new[2, :, cs] = v
        return carry

    lax.fori_loop(0, chunks, do_chunk, 0)

    gain_outs = [
        pltpu.make_async_copy(gains_new.at[0], gain_out, out_sem.at[2]),
        pltpu.make_async_copy(gains_new.at[1], gfirst_out, out_sem.at[3]),
        pltpu.make_async_copy(gains_new.at[2], gsecond_out, out_sem.at[4]),
    ]
    for out in gain_outs:
        out.start()

    for owner in range(n_f):

        @pl.when(jnp.logical_and(me_f >= owner, me_f < n_f - 1))
        def _(owner=owner):
            key_copy(owner, 1).wait_send()

        @pl.when(jnp.logical_and(me_f <= owner, me_f > 0))
        def _(owner=owner):
            key_copy(owner, -1).wait_send()


    def drain(j, carry):
        for offset in offsets:
            act_copy(offset, j).wait_send()
        merged_copy(j).wait()
        return carry

    for c in range(chips):
        pair_copy(c).wait_send()
        fw_copy(c, me_r).wait_send()
    for offset in range(1, chips):
        rs_copy(offset).wait_send()
        ag_copy(offset, me_r, peer_chip(offset) * 2 + core).wait_send()
    lax.fori_loop(0, chunks, drain, 0)
    for out in outs + gain_outs:
        out.wait()


def hand_over(*refs):
    sources, targets, buffers, (in_sem, out_sem) = refs[:6], refs[6:12], refs[12:18], refs[18:]
    features = sources[0].shape[1]
    pieces = [(0, (0, pl.ds(i * (features // 4), features // 4))) for i in range(4)]
    pieces += [(i, (slice(None),)) for i in range(1, 6)]
    moves = []
    for n, (i, at) in enumerate(pieces):
        moves.append((
            pltpu.make_async_copy(sources[i].at[at], buffers[i].at[at], in_sem.at[n]),
            pltpu.make_async_copy(buffers[i].at[at], targets[i].at[at], out_sem.at[n]),
        ))
    for load, _ in moves:
        load.start()
    for load, store in moves:
        load.wait()
        store.start()
    for _, store in moves:
        store.wait()


def shards(
    n_f,
    n_r,
    activations,
    key_grad,
    inner_weight,
    weight_first,
    weight_second,
    norm_gain,
    gain_first,
    gain_second,
    step_count,
    outer_params,
    outer_momentum,
):
    tokens, width = activations.shape[1:]
    features, cols = inner_weight.shape[1:]
    rows = outer_params.shape[0]
    chips = n_r // 2
    chunk = min(256, cols)
    chunks = cols // chunk
    dma = pltpu.SemaphoreType.DMA
    any_spec = pl.BlockSpec(memory_space=pl.ANY)
    results = pl.pallas_call(
        functools.partial(kernel, n_f, n_r, chunk),
        out_shape=(
            jax.ShapeDtypeStruct(inner_weight.shape, BF16),
            jax.ShapeDtypeStruct(outer_params.shape, F32),
            jax.ShapeDtypeStruct(outer_params.shape, F32),
            jax.ShapeDtypeStruct(norm_gain.shape, F32),
            jax.ShapeDtypeStruct(norm_gain.shape, F32),
            jax.ShapeDtypeStruct(norm_gain.shape, F32),
        ),
        in_specs=[pl.BlockSpec(memory_space=pltpu.SMEM)] + [any_spec] * 10,
        out_specs=(any_spec,) * 6,
        scratch_shapes=[
            pltpu.VMEM((tokens, width), BF16),
            pltpu.VMEM((n_f * tokens, cols), BF16),
            pltpu.VMEM((tokens, features), BF16),
            pltpu.VMEM((tokens, features), F32),
            pltpu.VMEM((features, n_f * tokens), BF16),
            pltpu.VMEM((features, cols), BF16),
            pltpu.VMEM((features, cols), BF16),
            pltpu.VMEM((features, cols), BF16),
            pltpu.VMEM((features, chunk), F32),
            pltpu.VMEM((features, cols), BF16),
            pltpu.VMEM((chips, rows, cols), BF16),
            pltpu.VMEM((chips, rows, cols), BF16),
            pltpu.VMEM((chips, rows, cols), BF16),
            pltpu.VMEM((features, cols), BF16),
            pltpu.VMEM((rows, cols), F32),
            pltpu.VMEM((rows, cols), F32),
            pltpu.VMEM((rows, cols), F32),
            pltpu.VMEM((rows, cols), F32),
            pltpu.VMEM((3, 1, cols), F32),
            pltpu.VMEM((3, 1, cols), F32),
            dma((11,)),
            dma((5 + chunks,)),
            dma((n_f - 1, chunks)),
            dma((n_f - 1, chunks)),
            dma((2, n_f)),
            dma((n_f,)),
            dma((chips,)),
            dma((chips,)),
            dma((chips - 1,)),
            dma((chips - 1,)),
            dma((chips - 1,)),
            dma((chips - 1,)),
            dma((chips,)),
            dma((chips,)),
        ],
        compiler_params=pltpu.CompilerParams(
            collective_id=0, has_side_effects=True, vmem_limit_bytes=VMEM_LIMIT
        ),
        name="diloco_step",
    )(
        step_count.reshape(1),
        activations,
        key_grad,
        inner_weight,
        weight_first,
        weight_second,
        norm_gain,
        gain_first,
        gain_second,
        outer_params,
        outer_momentum,
    )
    return pl.pallas_call(
        hand_over,
        out_shape=tuple(jax.ShapeDtypeStruct(r.shape, r.dtype) for r in results),
        in_specs=[any_spec] * 6,
        out_specs=(any_spec,) * 6,
        scratch_shapes=[pltpu.VMEM(r.shape, r.dtype) for r in results] + [dma((9,)), dma((9,))],
        compiler_params=pltpu.CompilerParams(vmem_limit_bytes=VMEM_LIMIT),
        name="hand_over",
    )(*results)


def solution(mesh):
    return jax.shard_map(
        functools.partial(shards, mesh.shape["fsdp"], mesh.shape["replica"]),
        mesh=mesh,
        in_specs=(
            P("replica", "fsdp", None),
            P("replica", "fsdp", None),
            P("replica", None, "fsdp"),
            P("replica", None, "fsdp"),
            P("replica", None, "fsdp"),
            P("replica", "fsdp"),
            P("replica", "fsdp"),
            P("replica", "fsdp"),
            P(),
            P("replica", "fsdp"),
            P("replica", "fsdp"),
        ),
        out_specs=(
            P("replica", None, "fsdp"),
            P("replica", "fsdp"),
            P("replica", "fsdp"),
            P("replica", "fsdp"),
            P("replica", "fsdp"),
            P("replica", "fsdp"),
        ),
        check_vma=False,
    )
```
